512 devices in a mesh: row: 32 (over z, y_hi, core), col: 16 (over x, y_lo).
Axes of the slice: x: 4, y: 8 (y_hi: 2, y_lo: 4; y = y_hi * 4 + y_lo), z: 8, core: 2. Of those that a mesh axis runs over, the one named last changes fastest.
Arguments:
- density: bfloat16 [64, 48, 128, 128], P('row', 'col'), as said below
- block_cols: int32 [64, 48], P('row', 'col'), may hold values from 0 to 63, as said below
- block_counts: int32 [64, 16], P('row', 'col'), may hold values from 0 to 3, as said below
Outputs:
- purified: bfloat16 [64, 48, 128, 128], P('row', 'col')
The draws below stay inside these ranges and needn't reach their ends.
Inputs may be any that keep to these rules, and one draw needn't show every extreme that they name: The 3 slots c*3 to c*3 + 2 of block_cols[i] name distinct block-columns of group c, that is of [c*4, (c+1)*4); the first block_counts[i, c] of them are live, the rest are padding. The pattern is symmetric: column j is live in block-row i exactly when column i is live in block-row j; column i is always live in block-row i. `block_counts`: every block-row has 3 live slots in the group that holds its own index. `density`: P is symmetric: the live block of block-row i at column j equals the transpose of the live block of block-row j at column i. Padding slots hold arbitrary finite values.
All inputs are finite; a program needn't handle non-finite values.
Results may differ from the reference program's by a relative error of at most 0.0041.
Values may be sent and summed in bfloat16 or wider, within the bound.
No kernel may reach another device: no remote copies, remote signals or barrier semaphores. Data moves between devices by JAX's collectives and lax.ppermute only.
A program may use at most 64 MiB of HBM per device.

```python
import math
import jax
import jax.numpy as jnp
from jax import lax

BS = 128
KD = 3
NB = 64
CG = 4
SLOTS = 48
N_COL = 16


def pattern_layout(key):
    key_shift, key_pairs = jax.random.split(key, 2)
    group_ids = jnp.arange(N_COL, dtype=jnp.int32)
    shift_table = jax.random.randint(key_shift, (N_COL, N_COL), 0, CG, dtype=jnp.int32)
    lower_half = group_ids[:, None] <= group_ids[None, :]
    shift_table = jnp.where(lower_half, shift_table, shift_table.T)
    same_group = group_ids[:, None] == group_ids[None, :]
    shift_table = jnp.where(same_group, 0, shift_table)
    offsets = jnp.bitwise_xor(shift_table[:, :, None], jnp.arange(KD, dtype=jnp.int32)[None, None, :])
    row_ids = jnp.arange(NB, dtype=jnp.int32)
    home_group = row_ids // CG
    local_index = row_ids % CG
    canonical = group_ids[None, :, None] * CG + jnp.bitwise_xor(local_index[:, None, None], offsets[home_group])
    pair_bits = jax.random.randint(key_pairs, (NB, NB), 0, 2, dtype=jnp.int32)
    pair_low = jnp.minimum(row_ids[:, None, None], canonical)
    pair_high = jnp.maximum(row_ids[:, None, None], canonical)
    live_mask = (pair_bits[pair_low, pair_high] == 0) | (group_ids[None, :, None] == home_group[:, None, None])
    slot_order = jnp.argsort(jnp.where(live_mask, 0, 1), axis=2, stable=True).astype(jnp.int32)
    return (canonical, live_mask, slot_order, home_group)


def draw_block_cols(key, part):
    canonical, live_mask, slot_order, home_group = pattern_layout(key)
    columns = jnp.take_along_axis(canonical, slot_order, axis=2)
    return columns.reshape(NB, N_COL * KD).astype(jnp.int32)


def draw_block_counts(key, part):
    canonical, live_mask, slot_order, home_group = pattern_layout(key)
    return jnp.sum(live_mask.astype(jnp.int32), axis=2).astype(jnp.int32)


def draw_density(key, part):
    canonical, live_mask, slot_order, home_group = pattern_layout(key)
    key = jax.random.fold_in(key, 11)
    key_blocks = jax.random.fold_in(key, 0)
    block_shape = (NB, N_COL, KD, BS, BS)
    base_blocks = jax.random.normal(key_blocks, block_shape, jnp.float32)
    slot_ids = jnp.arange(KD, dtype=jnp.int32)
    partner = base_blocks[canonical, home_group[:, None, None], slot_ids[None, None, :]]
    blocks = (base_blocks + jnp.swapaxes(partner, 3, 4)) * (0.1 / math.sqrt(2.0))
    row_ids = jnp.arange(NB, dtype=jnp.int32)
    group_ids = jnp.arange(N_COL, dtype=jnp.int32)
    arranged = blocks[row_ids[:, None, None], group_ids[None, :, None], slot_order]
    return arranged.reshape(NB, N_COL * KD, BS, BS).astype(jnp.bfloat16)


def setup_inputs(seed: int = 0) -> dict:
    seeds = jax.random.split(jax.random.key(seed), 4)
    density = draw_density(jax.random.fold_in(seeds[3], 71), 0)
    block_cols = draw_block_cols(jax.random.fold_in(seeds[3], 71), 0)
    block_counts = draw_block_counts(jax.random.fold_in(seeds[3], 71), 0)
    return {"density": density, "block_cols": block_cols, "block_counts": block_counts}


def live_slots(block_counts):
    slot_ids = jnp.arange(SLOTS, dtype=jnp.int32)
    return (slot_ids % KD)[None, :] < jnp.repeat(block_counts, KD, axis=1)


def restricted_product(left_blocks, right_blocks, block_cols, live_mask):
    right_cols = block_cols.reshape(NB, N_COL, KD)
    right_live = live_mask.reshape(NB, N_COL, KD)

    def one_row(row_items):
        left_row, cols_row, live_row = row_items
        picked = right_blocks[cols_row].reshape(SLOTS, N_COL, KD, BS, BS).astype(jnp.float32)
        picked_cols = right_cols[cols_row]
        picked_live = right_live[cols_row]
        target_cols = cols_row.reshape(N_COL, KD)
        target_live = live_row.reshape(N_COL, KD)
        matches = picked_cols[:, :, :, None] == target_cols[None, :, None, :]
        matches = matches & picked_live[:, :, :, None] & live_row[:, None, None, None] & target_live[None, :, None, :]
        chosen = jnp.einsum("agtu,agtxy->aguxy", matches.astype(jnp.float32), picked)
        product = jnp.einsum("axy,aguyz->guxz", left_row.astype(jnp.float32), chosen)
        return product.reshape(SLOTS, BS, BS)

    return lax.map(one_row, (left_blocks, block_cols, live_mask))


def reference(density, block_cols, block_counts):
    live_mask = live_slots(block_counts)
    square = restricted_product(density, density, block_cols, live_mask)
    square_low = square.astype(jnp.bfloat16)
    cube_sums = restricted_product(square_low, density, block_cols, live_mask)
    return (3.0 * square - 2.0 * cube_sums).astype(jnp.bfloat16)
```

```python
import jax
import jax.numpy as jnp
from jax import lax
from jax.experimental import pallas as pl
from jax.experimental.pallas import tpu as pltpu
from jax.sharding import PartitionSpec as P

BS = 128
KD = 3
CG = 4
ROWS = 2
NG = 16
BLK = ROWS * KD * BS
PAY = BLK + 16
BF = jnp.bfloat16
F32 = jnp.float32

CORE_SWAP = [(r, r ^ 1) for r in range(32)]
YH_SWAP = [(r, r ^ 2) for r in range(32)]
Z_STEP = [(r, (r + (4 if r % 2 == 0 else 28)) % 32) for r in range(32)]


def yl_shift(s):
    return [(c, c // 4 * 4 + (c + s) % 4) for c in range(16)]


def x_shift(s):
    return [(c, (c + 4 * s) % 16) for c in range(16)]


def col_gather(own, rows):
    pieces = [own] + [lax.ppermute(own, "col", yl_shift(s)) for s in (1, 3, 2)]
    line = jnp.concatenate(pieces, axis=0)
    left = lax.ppermute(line, "col", x_shift(1))
    right = lax.ppermute(line, "col", x_shift(3))
    far_lo = lax.ppermute(left[: 2 * rows], "col", x_shift(1))
    far_hi = lax.ppermute(right[2 * rows :], "col", x_shift(3))
    return [line, left, right, far_lo, far_hi]


COL_PIECES = (
    [(0, n, 0, o) for n, o in enumerate((0, 3, 1, 2))]
    + [(1, n, 3, o) for n, o in enumerate((0, 3, 1, 2))]
    + [(2, n, 1, o) for n, o in enumerate((0, 3, 1, 2))]
    + [(3, 0, 2, 0), (3, 1, 2, 3), (4, 0, 2, 1), (4, 1, 2, 2)]
)


def row_gather(own):
    other = lax.ppermute(own, "row", CORE_SWAP)
    own_y = lax.ppermute(own, "row", YH_SWAP)
    other_y = lax.ppermute(own_y, "row", CORE_SWAP)
    out = []
    for pair in ((own, other), (own_y, other_y)):
        current = jnp.concatenate(pair, axis=0)
        ring = [current]
        for step in range(4):
            current = lax.ppermute(current if step < 3 else current[:PAY], "row", Z_STEP)
            ring.append(current)
        out.append(ring)
    swapped = [[lax.ppermute(a, "row", CORE_SWAP) for a in ring[1:]] for ring in out]
    arrays, pieces = [], []
    for yh in range(2):
        for step in range(5):
            for n in range(1 if step == 4 else 2):
                pieces.append((len(arrays), n, step, yh, n))
            arrays.append(out[yh][step])
        for step in range(1, 5):
            for n in range(1 if step == 4 else 2):
                pieces.append((len(arrays), n, -step, yh, 1 - n))
            arrays.append(swapped[yh][step - 1])
    return arrays, pieces


def meta_rows(meta):
    wide = meta.astype(F32)
    return [
        jnp.broadcast_to(wide[s : s + 1], (16, BS)).astype(BF) for s in range(ROWS * KD)
    ]


def spread(src, base, slots, store):
    masks = [[m == jnp.full((16, BS), q, BF) for q in range(CG)] for m in slots]

    def step(n, _):
        r = pl.multiple_of(n * 16, 16)
        v = [src[pl.ds(base + t * BS + r, 16), :] for t in range(KD)]
        zero = jnp.zeros((16, BS), BF)
        for q in range(CG):
            d = zero
            for t in range(KD):
                d = jnp.where(masks[t][q], v[t], d)
            store(r, q, d)
        return 0

    lax.fori_loop(0, BS // 16, step, 0, unroll=True)


def spread_strip(src, piece, rows, meta, group, a_ref):
    slots = meta_rows(meta)
    for i in range(ROWS):

        def store(r, q, d, i=i):
            col = pl.multiple_of(group * (CG * BS) + q * BS, BS)
            a_ref[pl.ds(i * BS + r, 16), pl.ds(col, BS)] = d

        spread(src, piece * rows + i * KD * BS, slots[i * KD : (i + 1) * KD], store)


def dot(a_ref, b_ref):
    return jnp.dot(a_ref[...], b_ref[...], preferred_element_type=F32)


def pick(acc, slots):
    out = []
    for i in range(ROWS):
        for t in range(KD):
            m = slots[i * KD + t].astype(F32)[0:1]
            d = jnp.zeros((BS, BS), F32)
            for q in range(CG):
                d = jnp.where(m == float(q), acc[i * BS : (i + 1) * BS, q * BS : (q + 1) * BS], d)
            out.append(d)
    return out


def square_kernel(n_col, row_pieces, pos, *refs):
    cols, rows = refs[:n_col], refs[n_col:-5]
    square_ref, low_ref, b_ref, meta_ref, a_ref = refs[-5:]
    z, yh, core, x, yl = (pos[n] for n in range(5))
    sign = 1 - 2 * core
    for n, (arr, piece, dx, dy) in enumerate(COL_PIECES):
        src = cols[arr]
        group = ((x + dx) & 3) * 4 + ((yl + dy) & 3)
        meta = src[piece * PAY + BLK : (piece + 1) * PAY]
        meta_ref[n * 16 : (n + 1) * 16] = meta
        spread_strip(src, piece, PAY, meta, group, a_ref)
    for arr, piece, step, dyh, dcore in row_pieces:
        src = rows[arr]
        group = ((z - sign * step) & 7) * 2 + (yh ^ dyh)
        slots = meta_rows(src[piece * PAY + BLK : (piece + 1) * PAY])
        for i in range(ROWS):
            top = pl.multiple_of((group * CG + (core ^ dcore) * 2 + i) * BS, BS)

            def store(r, q, d, top=top):
                b_ref[pl.ds(top + r, 16), q * BS : (q + 1) * BS] = d

            spread(src, piece * PAY + i * KD * BS, slots[i * KD : (i + 1) * KD], store)
    own = meta_rows(cols[0][BLK:PAY])
    for s, d in enumerate(pick(dot(a_ref, b_ref), own)):
        square_ref[s * BS : (s + 1) * BS] = d
        low_ref[s * BS : (s + 1) * BS] = d.astype(BF)


def cube_kernel(pos, meta_ref, b_ref, square_ref, *refs):
    cols, (out_ref, a_ref) = refs[:-2], refs[-2:]
    x, yl = pos[3], pos[4]
    for n, (arr, piece, dx, dy) in enumerate(COL_PIECES):
        group = ((x + dx) & 3) * 4 + ((yl + dy) & 3)
        spread_strip(cols[arr], piece, BLK, meta_ref[n * 16 : (n + 1) * 16], group, a_ref)
    own = meta_rows(meta_ref[0:16])
    for s, d in enumerate(pick(dot(a_ref, b_ref), own)):
        square = square_ref[s * BS : (s + 1) * BS]
        out_ref[s * BS : (s + 1) * BS] = (3.0 * square - 2.0 * d).astype(BF)


VM = pl.BlockSpec(memory_space=pltpu.VMEM)
SM = pl.BlockSpec(memory_space=pltpu.SMEM)
PARAMS = pltpu.CompilerParams(vmem_limit_bytes=36 * 1024 * 1024)


def local(density, block_cols, block_counts):
    slot = lax.broadcasted_iota(jnp.int32, (ROWS, KD), 1)
    where = jnp.where(slot < block_counts, block_cols % CG, -1).reshape(ROWS * KD, 1)
    meta = jnp.broadcast_to(where, (ROWS * KD, BS)).astype(BF)
    own = jnp.concatenate(
        [density.reshape(BLK, BS), meta, jnp.zeros((16 - ROWS * KD, BS), BF)], axis=0
    )
    r, c = lax.axis_index("row"), lax.axis_index("col")
    pos = jnp.stack([r // 4, r // 2 % 2, r % 2, c // 4, c % 4]).astype(jnp.int32)
    cols = col_gather(own, PAY)
    rows, row_pieces = row_gather(own)

    def call(pos, *arrays):
        return square_kernel(len(cols), row_pieces, pos, *arrays)

    square, low, b, metas = pl.pallas_call(
        call,
        out_shape=[
            jax.ShapeDtypeStruct((BLK, BS), F32),
            jax.ShapeDtypeStruct((BLK, BS), BF),
            jax.ShapeDtypeStruct((NG * CG * BS, CG * BS), BF),
            jax.ShapeDtypeStruct((NG * 16, BS), BF),
        ],
        in_specs=[SM] + [VM] * (len(cols) + len(rows)),
        out_specs=[VM] * 4,
        scratch_shapes=[pltpu.VMEM((ROWS * BS, NG * CG * BS), BF)],
        compiler_params=PARAMS,
        name="square",
    )(pos, *cols, *rows)
    lows = col_gather(low, BLK)
    out = pl.pallas_call(
        cube_kernel,
        out_shape=jax.ShapeDtypeStruct((BLK, BS), BF),
        in_specs=[SM] + [VM] * (3 + len(lows)),
        out_specs=VM,
        scratch_shapes=[pltpu.VMEM((ROWS * BS, NG * CG * BS), BF)],
        compiler_params=PARAMS,
        name="cube",
    )(pos, metas, b, square, *lows)
    return out.reshape(density.shape)


def solution(mesh):
    return jax.shard_map(
        local,
        mesh=mesh,
        in_specs=(P("row", "col", None, None), P("row", "col"), P("row", "col")),
        out_specs=P("row", "col", None, None),
        check_vma=False,
    )
```

```python
import jax
import jax.numpy as jnp
from jax import lax
from jax.experimental import pallas as pl
from jax.experimental.pallas import tpu as pltpu
from jax.sharding import PartitionSpec as P

BS = 128
KD = 3
CG = 4
ROWS = 2
NG = 16
BLK = ROWS * KD * BS
PAY = BLK + 16
BF = jnp.bfloat16
F32 = jnp.float32

VM = pl.BlockSpec(memory_space=pltpu.VMEM)
SM = pl.BlockSpec(memory_space=pltpu.SMEM)

CORE_SWAP = [(r, r ^ 1) for r in range(32)]
YH_SWAP = [(r, r ^ 2) for r in range(32)]
Z_STEP = [(r, (r + (4 if r % 2 == 0 else 28)) % 32) for r in range(32)]


def yl_shift(s):
    return [(c, c // 4 * 4 + (c + s) % 4) for c in range(16)]


def x_shift(s):
    return [(c, (c + 4 * s) % 16) for c in range(16)]


Z_FAR = [(r, (r + 16) % 32) for r in range(32)]


def fence(token, *values):
    token, *values = lax.optimization_barrier((token, *values))

    def body(in_ref, out_ref):
        out_ref[...] = in_ref[...]

    token = pl.pallas_call(
        body,
        out_shape=jax.ShapeDtypeStruct(token.shape, token.dtype),
        in_specs=[VM],
        out_specs=VM,
        compiler_params=pltpu.CompilerParams(vmem_limit_bytes=1024 * 1024),
        cost_estimate=pl.CostEstimate(flops=50 * 10**9, bytes_accessed=0, transcendentals=0),
        name="fence",
    )(token)
    return lax.optimization_barrier((token, *values))


def cat(*arrays):
    rows = [a.shape[0] for a in arrays]

    def body(*refs):
        at = 0
        for n, ref in zip(rows, refs):
            refs[-1][at : at + n] = ref[...]
            at += n

    return pl.pallas_call(
        body,
        out_shape=jax.ShapeDtypeStruct((sum(rows), BS), BF),
        in_specs=[VM] * len(arrays),
        out_specs=VM,
        compiler_params=pltpu.CompilerParams(vmem_limit_bytes=2 * 1024 * 1024),
        name="cat",
    )(*arrays)


def gather_all(own):
    def row(a, perm):
        return lax.ppermute(a, "row", perm)

    def col(a, perm):
        return lax.ppermute(a, "col", perm)

    tok = jnp.zeros((8, BS), F32)
    other = row(own, CORE_SWAP)
    own_y = row(own, YH_SWAP)
    line1 = col(own, yl_shift(1))
    w0 = cat(own, other)
    tok, w0, own = fence(tok, w0, own)
    w1 = row(w0, Z_STEP)
    line3 = col(own, yl_shift(3))
    line2 = col(own, yl_shift(2))
    one = cat(own, line1)
    other_y = row(own_y, CORE_SWAP)
    v0 = cat(own_y, other_y)
    tok, v0, one, own_y = fence(tok, v0, one, own_y)
    v1 = row(v0, Z_STEP)
    left1, right1 = col(one, x_shift(1)), col(one, x_shift(3))
    w2 = row(w1, Z_STEP)
    two = cat(line3, line2)
    tok, two, w1, w2, own_y = fence(tok, two, w1, w2, own_y)
    far_y = row(own_y, Z_FAR)
    left2, right2 = col(two, x_shift(1)), col(two, x_shift(3))
    v2 = row(v1, Z_STEP)
    w3 = row(w2, Z_STEP)
    tok, left1, right1, v1, v2 = fence(tok, left1, right1, v1, v2)
    far1, far2 = col(left1[:PAY], x_shift(1)), col(right1[PAY:], x_shift(3))
    v3 = row(v2, Z_STEP)
    w4 = row(w3[:PAY], Z_STEP)
    tok, left2, right2, far_y, w3 = fence(tok, left2, right2, far_y, w3)
    far3, far4 = col(left2[:PAY], x_shift(1)), col(right2[PAY:], x_shift(3))
    ws = cat(w1, w2, w3, w4)
    ws_other = row(ws, CORE_SWAP)
    vs = cat(v1, v2, far_y, v3)
    vs_other = row(vs, CORE_SWAP)
    rows = [w0, v0, ws, ws_other, vs, vs_other]
    pieces = [(yh, n, 0, yh, n) for yh in range(2) for n in range(2)]
    for n, (step, c) in enumerate(((1, 0), (1, 1), (2, 0), (2, 1), (3, 0), (3, 1), (4, 0))):
        pieces += [(2, n, step, 0, c), (3, n, -step, 0, 1 - c)]
    for n, (step, c) in enumerate(((1, 0), (1, 1), (2, 0), (2, 1), (4, 0), (3, 0), (3, 1))):
        pieces += [(4, n, step, 1, c), (5, n, -step, 1, 1 - c)]
    return [one, left1, right1, two, left2, right2, far1, far2, far3, far4], rows, pieces


def col_gather(own, rows):
    near = [lax.ppermute(own, "col", yl_shift(s)) for s in (1, 3, 2)]
    one = jnp.concatenate([own, near[0]], axis=0)
    left1 = lax.ppermute(one, "col", x_shift(1))
    right1 = lax.ppermute(one, "col", x_shift(3))
    two = jnp.concatenate(near[1:], axis=0)
    left2 = lax.ppermute(two, "col", x_shift(1))
    right2 = lax.ppermute(two, "col", x_shift(3))
    far1 = lax.ppermute(left1[:rows], "col", x_shift(1))
    far2 = lax.ppermute(right1[rows:], "col", x_shift(3))
    far3 = lax.ppermute(left2[:rows], "col", x_shift(1))
    far4 = lax.ppermute(right2[rows:], "col", x_shift(3))
    return [one, left1, right1, two, left2, right2, far1, far2, far3, far4]


COL_PIECES = (
    [(a, n, dx, dy) for a, dx in ((0, 0), (1, 3), (2, 1)) for n, dy in ((0, 0), (1, 3))]
    + [(a, n, dx, dy) for a, dx in ((3, 0), (4, 3), (5, 1)) for n, dy in ((0, 1), (1, 2))]
    + [(6, 0, 2, 0), (7, 0, 2, 3), (8, 0, 2, 1), (9, 0, 2, 2)]
)


def meta_rows(meta):
    wide = meta.astype(F32)
    return [
        jnp.broadcast_to(wide[s : s + 1], (16, BS)).astype(BF) for s in range(ROWS * KD)
    ]


def spread(src, base, slots, store):
    masks = [[m == jnp.full((16, BS), q, BF) for q in range(CG)] for m in slots]

    def step(n, _):
        r = pl.multiple_of(n * 16, 16)
        v = [src[pl.ds(base + t * BS + r, 16), :] for t in range(KD)]
        zero = jnp.zeros((16, BS), BF)
        for q in range(CG):
            d = zero
            for t in range(KD):
                d = jnp.where(masks[t][q], v[t], d)
            store(r, q, d)
        return 0

    lax.fori_loop(0, BS // 16, step, 0, unroll=True)


def spread_strip(src, piece, rows, meta, group, a_ref):
    slots = meta_rows(meta)
    for i in range(ROWS):

        def store(r, q, d, i=i):
            col = pl.multiple_of(group * (CG * BS) + q * BS, BS)
            a_ref[pl.ds(i * BS + r, 16), pl.ds(col, BS)] = d

        spread(src, piece * rows + i * KD * BS, slots[i * KD : (i + 1) * KD], store)


def dot(a_ref, b_ref):
    return jnp.dot(a_ref[...], b_ref[...], preferred_element_type=F32)


def pick(acc, slots):
    out = []
    for i in range(ROWS):
        for t in range(KD):
            m = slots[i * KD + t].astype(F32)[0:1]
            d = jnp.zeros((BS, BS), F32)
            for q in range(CG):
                d = jnp.where(m == float(q), acc[i * BS : (i + 1) * BS, q * BS : (q + 1) * BS], d)
            out.append(d)
    return out


def fetch(arrays, buffers, sems):
    copies = [pltpu.make_async_copy(a, b, sems.at[n]) for n, (a, b) in enumerate(zip(arrays, buffers))]
    for copy in copies:
        copy.start()
    return copies


def group_of(x, yl, dx, dy):
    return ((x + dx) & 3) * 4 + ((yl + dy) & 3)


def square_kernel(n_col, n_row, row_pieces, pos, *refs):
    arrays, rest = refs[: n_col + n_row], refs[n_col + n_row :]
    square_ref, low_ref, b_out, meta_ref, a_ref, b_ref = rest[:6]
    buffers, sems, b_sem = rest[6:-2], rest[-2], rest[-1]
    copies = fetch(arrays, buffers, sems)
    cols, rows = buffers[:n_col], buffers[n_col:]
    z, yh, core, x, yl = (pos[n] for n in range(5))
    sign = 1 - 2 * core
    for arr in range(n_row):
        copies[n_col + arr].wait()
        for piece, step, dyh, dcore in [p[1:] for p in row_pieces if p[0] == arr]:
            src = rows[arr]
            group = ((z - sign * step) & 7) * 2 + (yh ^ dyh)
            slots = meta_rows(src[piece * PAY + BLK : (piece + 1) * PAY])
            for i in range(ROWS):
                top = pl.multiple_of((group * CG + (core ^ dcore) * 2 + i) * BS, BS)

                def store(r, q, d, top=top):
                    b_ref[pl.ds(top + r, 16), q * BS : (q + 1) * BS] = d

                spread(src, piece * PAY + i * KD * BS, slots[i * KD : (i + 1) * KD], store)
    b_copy = pltpu.make_async_copy(b_ref, b_out, b_sem)
    b_copy.start()
    for arr in range(n_col):
        copies[arr].wait()
        for n, (a, piece, dx, dy) in enumerate(COL_PIECES):
            if a == arr:
                src = cols[arr]
                meta = src[piece * PAY + BLK : (piece + 1) * PAY]
                at = pl.multiple_of(group_of(x, yl, dx, dy) * 16, 16)
                meta_ref[pl.ds(at, 16), :] = meta
                spread_strip(src, piece, PAY, meta, group_of(x, yl, dx, dy), a_ref)
    own = meta_rows(cols[0][BLK:PAY])
    for s, d in enumerate(pick(dot(a_ref, b_ref), own)):
        square_ref[s * BS : (s + 1) * BS] = d
        low_ref[s * BS : (s + 1) * BS] = d.astype(BF)
    b_copy.wait()


def cube_kernel(n_col, pos, meta_ref, square_ref, b_in, *refs):
    arrays, rest = refs[:n_col], refs[n_col:]
    out_ref, a_ref, b_ref, buffers, sems = rest[0], rest[1], rest[2], rest[3:-1], rest[-1]
    copies = fetch((b_in, *arrays), (b_ref, *buffers), sems)
    x, yl = pos[3], pos[4]
    for arr in range(n_col):
        copies[1 + arr].wait()
        for a, piece, dx, dy in COL_PIECES:
            if a == arr:
                group = group_of(x, yl, dx, dy)
                meta = meta_ref[pl.ds(pl.multiple_of(group * 16, 16), 16), :]
                spread_strip(buffers[arr], piece, BLK, meta, group, a_ref)
    copies[0].wait()
    at = pl.multiple_of(group_of(x, yl, 0, 0) * 16, 16)
    own = meta_rows(meta_ref[pl.ds(at, 16), :])
    for s, d in enumerate(pick(dot(a_ref, b_ref), own)):
        square = square_ref[s * BS : (s + 1) * BS]
        out_ref[s * BS : (s + 1) * BS] = (3.0 * square - 2.0 * d).astype(BF)


HB = pl.BlockSpec(memory_space=pl.ANY)
PARAMS = pltpu.CompilerParams(vmem_limit_bytes=56 * 1024 * 1024)
A_SCRATCH = pltpu.VMEM((ROWS * BS, NG * CG * BS), BF)
B_SHAPE = (NG * CG * BS, CG * BS)


def local(density, block_cols, block_counts):
    slot = lax.broadcasted_iota(jnp.int32, (ROWS, KD), 1)
    where = jnp.where(slot < block_counts, block_cols % CG, -1).reshape(ROWS * KD, 1)
    meta = jnp.broadcast_to(where, (ROWS * KD, BS)).astype(BF)
    own = jnp.concatenate(
        [density.reshape(BLK, BS), meta, jnp.zeros((16 - ROWS * KD, BS), BF)], axis=0
    )
    r, c = lax.axis_index("row"), lax.axis_index("col")
    pos = jnp.stack([r // 4, r // 2 % 2, r % 2, c // 4, c % 4]).astype(jnp.int32)
    cols, rows, row_pieces = gather_all(own)

    def square_call(pos, *refs):
        square_kernel(len(cols), len(rows), row_pieces, pos, *refs)

    square, low, b, metas = pl.pallas_call(
        square_call,
        out_shape=[
            jax.ShapeDtypeStruct((BLK, BS), F32),
            jax.ShapeDtypeStruct((BLK, BS), BF),
            jax.ShapeDtypeStruct(B_SHAPE, BF),
            jax.ShapeDtypeStruct((NG * 16, BS), BF),
        ],
        in_specs=[SM] + [HB] * (len(cols) + len(rows)),
        out_specs=[VM, VM, HB, VM],
        scratch_shapes=[A_SCRATCH, pltpu.VMEM(B_SHAPE, BF)]
        + [pltpu.VMEM(a.shape, BF) for a in cols + rows]
        + [pltpu.SemaphoreType.DMA((len(cols) + len(rows),)), pltpu.SemaphoreType.DMA(())],
        compiler_params=PARAMS,
        name="square",
    )(pos, *cols, *rows)
    lows = col_gather(low, BLK)

    def cube_call(pos, *refs):
        cube_kernel(len(lows), pos, *refs)

    out = pl.pallas_call(
        cube_call,
        out_shape=jax.ShapeDtypeStruct((BLK, BS), BF),
        in_specs=[SM, VM, VM, HB] + [HB] * len(lows),
        out_specs=VM,
        scratch_shapes=[A_SCRATCH, pltpu.VMEM(B_SHAPE, BF)]
        + [pltpu.VMEM(a.shape, BF) for a in lows]
        + [pltpu.SemaphoreType.DMA((1 + len(lows),))],
        compiler_params=PARAMS,
        name="cube",
    )(pos, metas, square, b, *lows)
    return out.reshape(density.shape)


def solution(mesh):
    return jax.shard_map(
        local,
        mesh=mesh,
        in_specs=(P("row", "col", None, None), P("row", "col"), P("row", "col")),
        out_specs=P("row", "col", None, None),
        check_vma=False,
    )
```

```python
import jax
import jax.numpy as jnp
from jax import lax
from jax.experimental import pallas as pl
from jax.experimental.pallas import tpu as pltpu
from jax.sharding import PartitionSpec as P

BS = 128
KD = 3
CG = 4
ROWS = 2
NG = 16
NZ = 8
BLK = ROWS * KD * BS
PAY = BLK + 16
HALF = NG * ROWS * BS
BF = jnp.bfloat16
F32 = jnp.float32
VM = pl.BlockSpec(memory_space=pltpu.VMEM)
SM = pl.BlockSpec(memory_space=pltpu.SMEM)
HBM = pl.BlockSpec(memory_space=pltpu.HBM)

CORE_SWAP = [(r, r ^ 1) for r in range(32)]
YH_SWAP = [(r, r ^ 2) for r in range(32)]
Z_GROUPS = [[z * 4 + n for z in range(NZ)] for n in range(4)]


def yl_shift(s):
    return [(c, c // 4 * 4 + (c + s) % 4) for c in range(16)]


def x_shift(s):
    return [(c, (c + 4 * s) % 16) for c in range(16)]


def col(a, perm):
    return lax.ppermute(a, "col", perm)


def row(a, perm):
    return lax.ppermute(a, "row", perm)


def shape(*dims, dtype=BF):
    return jax.ShapeDtypeStruct(dims, dtype)


def params(mib):
    return pltpu.CompilerParams(vmem_limit_bytes=mib * 1024 * 1024)


def fence(token, *values):
    token, *values = lax.optimization_barrier((token, *values))

    def body(in_ref, out_ref):
        out_ref[...] = in_ref[...]

    token = pl.pallas_call(
        body,
        out_shape=shape(*token.shape, dtype=token.dtype),
        in_specs=[VM],
        out_specs=VM,
        compiler_params=params(1),
        cost_estimate=pl.CostEstimate(flops=4 * 10**9, bytes_accessed=0, transcendentals=0),
        name="fence",
    )(token)
    return lax.optimization_barrier((token, *values))


def cat(*arrays):
    rows = [a.shape[0] for a in arrays]

    def body(*refs):
        at = 0
        for n, ref in zip(rows, refs):
            refs[-1][at : at + n] = ref[...]
            at += n

    return pl.pallas_call(
        body,
        out_shape=shape(sum(rows), BS),
        in_specs=[VM] * len(arrays),
        out_specs=VM,
        compiler_params=params(2),
        name="cat",
    )(*arrays)


X_FAR = x_shift(2)

ALL_PIECES = [
    (g * 4 + a, n, dx, dy)
    for g, dys in enumerate(((0, 3), (1, 2)))
    for a, dx in enumerate((0, 3, 1, 2))
    for n, dy in enumerate(dys)
]
NEAR_PIECES = [
    (g * 3 + a, n, dx, dy)
    for g, dys in enumerate(((0, 3), (1, 2)))
    for a, dx in enumerate((0, 3, 1))
    for n, dy in enumerate(dys)
]
FAR_PIECES = [(0, 0, 2, 0), (1, 0, 2, 3), (2, 0, 2, 1), (3, 0, 2, 2)]


def gather(own):
    token = jnp.zeros((8, BS), F32)
    own_y = row(own, YH_SWAP)
    one = cat(own, col(own, yl_shift(1)))
    token, one, own = fence(token, one, own)
    ones = [col(one, p) for p in (x_shift(1), x_shift(3), X_FAR)]
    token, both, own = fence(token, cat(own, own_y), own)
    column = lax.all_gather(both, "row", axis_index_groups=Z_GROUPS, axis=0, tiled=True)
    token, two = fence(token, cat(col(own, yl_shift(3)), col(own, yl_shift(2))))
    twos = [col(two, p) for p in (x_shift(1), x_shift(3), X_FAR)]
    return [one, *ones, two, *twos], column, token


def col_gather(own, rows):
    line1, line3, line2 = [col(own, yl_shift(s)) for s in (1, 3, 2)]
    one = cat(own, line1)
    left1, right1 = col(one, x_shift(1)), col(one, x_shift(3))
    two = cat(line3, line2)
    left2, right2 = col(two, x_shift(1)), col(two, x_shift(3))
    far1, far2 = col(left1[:rows], x_shift(1)), col(right1[rows:], x_shift(3))
    far3, far4 = col(left2[:rows], x_shift(1)), col(right2[rows:], x_shift(3))
    return [one, left1, right1, two, left2, right2], [far1, far2, far3, far4]


def meta_rows(meta):
    wide = meta.astype(F32)
    return [
        jnp.broadcast_to(wide[s : s + 1], (16, BS)).astype(BF) for s in range(ROWS * KD)
    ]


def spread(src, base, slots, store):
    masks = [[m == jnp.full((16, BS), q, BF) for q in range(CG)] for m in slots]

    def step(n, _):
        r = pl.multiple_of(n * 16, 16)
        v = [src[pl.ds(base + t * BS + r, 16), :] for t in range(KD)]
        zero = jnp.zeros((16, BS), BF)
        for q in range(CG):
            d = zero
            for t in range(KD):
                d = jnp.where(masks[t][q], v[t], d)
            store(r, q, d)
        return 0

    lax.fori_loop(0, BS // 16, step, 0, unroll=True)


def group_of(pos, dx, dy):
    return ((pos[3] + dx) & 3) * 4 + ((pos[4] + dy) & 3)


def spread_row(pos, src, base, i, slots, group, a_ref):
    def store(r, q, d):
        half = (q >> 1) ^ pos[2]
        at = pl.multiple_of(half * HALF + group * (ROWS * BS) + (q & 1) * BS, BS)
        a_ref[pl.ds(i * BS + r, 16), pl.ds(at, BS)] = d

    spread(src, base + i * KD * BS, slots[i * KD : (i + 1) * KD], store)


def pick(acc, slots):
    out = []
    for i in range(ROWS):
        for t in range(KD):
            m = slots[i * KD + t].astype(F32)[0:1]
            d = jnp.zeros((BS, BS), F32)
            for q in range(CG):
                d = jnp.where(m == float(q), acc[i * BS : (i + 1) * BS, q * BS : (q + 1) * BS], d)
            out.append(d)
    return out


def strip_kernel(pos, token, *refs):
    cols, (a_out, meta_ref, a_ref, sems) = refs[:-4], refs[-4:]
    copies = []
    for i in range(ROWS):
        for a, n, dx, dy in ALL_PIECES:
            src, group = cols[a], group_of(pos, dx, dy)
            meta = src[n * PAY + BLK : (n + 1) * PAY]
            if i == 0:
                meta_ref[pl.ds(pl.multiple_of(group * 16, 16), 16), :] = meta
            spread_row(pos, src, n * PAY, i, meta_rows(meta), group, a_ref)
        here = pl.ds(i * BS, BS)
        copies.append(pltpu.make_async_copy(a_ref.at[here], a_out.at[here], sems.at[i]))
        copies[-1].start()
    for copy in copies:
        copy.wait()


def fetch(src, buffer, sems):
    copies = []
    for z in range(NZ):
        part = pl.ds(z * 2 * PAY, 2 * PAY)
        copies.append(pltpu.make_async_copy(src.at[part], buffer.at[part], sems.at[z]))
        copies[-1].start()
    return copies


def half_kernel(pos, v_ref, b_ref, buffer, sems):
    copies = fetch(v_ref, buffer, sems)
    for z in range(NZ):
        copies[z].wait()
        for n in range(2):
            base = (z * 2 + n) * PAY
            slots = meta_rows(buffer[base + BLK : base + PAY])
            top = pl.multiple_of((z * 2 + (pos[1] ^ n)) * (ROWS * BS), ROWS * BS)
            for i in range(ROWS):

                def store(r, q, d, top=top + i * BS):
                    b_ref[pl.ds(top + r, 16), q * BS : (q + 1) * BS] = d

                spread(buffer, base + i * KD * BS, slots[i * KD : (i + 1) * KD], store)


def own_half_kernel(pos, a_in, v_ref, acc_ref, b_ref, buffer, sems, a_ref, a_sem):
    copy = pltpu.make_async_copy(a_in.at[:, pl.ds(0, HALF)], a_ref, a_sem)
    copy.start()
    half_kernel(pos, v_ref, b_ref, buffer, sems)
    copy.wait()
    acc_ref[...] = jnp.dot(a_ref[...], b_ref[...], preferred_element_type=F32)


def square_kernel(pos, meta_ref, acc_ref, a_in, v_ref, square_ref, low_ref, b_ref, buffer, sems, a_ref, a_sem):
    copy = pltpu.make_async_copy(a_in.at[:, pl.ds(HALF, HALF)], a_ref, a_sem)
    copy.start()
    half_kernel(pos, v_ref, b_ref, buffer, sems)
    copy.wait()
    acc = acc_ref[...] + jnp.dot(a_ref[...], b_ref[...], preferred_element_type=F32)
    at = pl.multiple_of(group_of(pos, 0, 0) * 16, 16)
    for s, d in enumerate(pick(acc, meta_rows(meta_ref[pl.ds(at, 16), :]))):
        square_ref[s * BS : (s + 1) * BS] = d
        low_ref[s * BS : (s + 1) * BS] = d.astype(BF)


def near_kernel(pos, meta_ref, b_own, b_other, *refs):
    lows, acc_ref, a_ref = refs[:-2], refs[-2], refs[-1]
    for _, _, dx, dy in FAR_PIECES:
        for half in range(2):
            at = pl.multiple_of(half * HALF + group_of(pos, dx, dy) * (ROWS * BS), ROWS * BS)
            a_ref[:, pl.ds(at, ROWS * BS)] = jnp.zeros((ROWS * BS, ROWS * BS), BF)
    for a, n, dx, dy in NEAR_PIECES:
        group = group_of(pos, dx, dy)
        meta = meta_ref[pl.ds(pl.multiple_of(group * 16, 16), 16), :]
        for i in range(ROWS):
            spread_row(pos, lows[a], n * BLK, i, meta_rows(meta), group, a_ref)
    acc_ref[...] = jnp.dot(a_ref[:, :HALF], b_own[...], preferred_element_type=F32) + jnp.dot(
        a_ref[:, HALF:], b_other[...], preferred_element_type=F32
    )


def far_kernel(pos, meta_ref, b_own, b_other, acc_ref, square_ref, *refs):
    lows, (out_ref, a_ref, b_ref) = refs[:-3], refs[-3:]
    width = ROWS * BS
    for m, (a, n, dx, dy) in enumerate(FAR_PIECES):
        group = group_of(pos, dx, dy)
        at = pl.multiple_of(group * width, width)
        for half, b in enumerate((b_own, b_other)):
            b_ref[(2 * m + half) * width : (2 * m + half + 1) * width] = b[pl.ds(at, width), :]
        slots = meta_rows(meta_ref[pl.ds(pl.multiple_of(group * 16, 16), 16), :])
        for i in range(ROWS):

            def store(r, q, d, i=i, m=m):
                half = (q >> 1) ^ pos[2]
                at = pl.multiple_of((2 * m + half) * width + (q & 1) * BS, BS)
                a_ref[pl.ds(i * BS + r, 16), pl.ds(at, BS)] = d

            spread(lows[a], n * BLK + i * KD * BS, slots[i * KD : (i + 1) * KD], store)
    acc = acc_ref[...] + jnp.dot(a_ref[...], b_ref[...], preferred_element_type=F32)
    at = pl.multiple_of(group_of(pos, 0, 0) * 16, 16)
    for s, d in enumerate(pick(acc, meta_rows(meta_ref[pl.ds(at, 16), :]))):
        square = square_ref[s * BS : (s + 1) * BS]
        out_ref[s * BS : (s + 1) * BS] = (3.0 * square - 2.0 * d).astype(BF)


def local(density, block_cols, block_counts):
    slot = lax.broadcasted_iota(jnp.int32, (ROWS, KD), 1)
    where = jnp.where(slot < block_counts, block_cols % CG, -1).reshape(ROWS * KD, 1)
    meta = jnp.broadcast_to(where, (ROWS * KD, BS)).astype(BF)
    meta = jnp.pad(meta, ((0, 16 - ROWS * KD), (0, 0)))
    density = density.reshape(BLK, BS)
    own = cat(density, meta)
    r, c = lax.axis_index("row"), lax.axis_index("col")
    pos = jnp.stack([r // 4, r // 2 % 2, r % 2, c // 4, c % 4]).astype(jnp.int32)
    strips, column, token = gather(own)
    acc_shape = shape(ROWS * BS, CG * BS, dtype=F32)
    b_shape = shape(HALF, CG * BS)
    a, metas = pl.pallas_call(
        strip_kernel,
        out_shape=[shape(ROWS * BS, 2 * HALF), shape(NG * 16, BS)],
        in_specs=[SM, VM] + [VM] * len(strips),
        out_specs=[HBM, VM],
        scratch_shapes=[pltpu.VMEM((ROWS * BS, 2 * HALF), BF), pltpu.SemaphoreType.DMA((ROWS,))],
        compiler_params=params(58),
        name="strips",
    )(pos, token, *strips)
    v, a, metas = lax.optimization_barrier((column, a, metas))
    v_other = row(v, CORE_SWAP)
    block_scratch = [
        pltpu.VMEM((2 * NZ * PAY, BS), BF),
        pltpu.SemaphoreType.DMA((NZ,)),
        pltpu.VMEM((ROWS * BS, HALF), BF),
        pltpu.SemaphoreType.DMA(()),
    ]
    acc, b_own = pl.pallas_call(
        own_half_kernel,
        out_shape=[acc_shape, b_shape],
        in_specs=[SM, HBM, HBM],
        out_specs=[VM, VM],
        scratch_shapes=block_scratch,
        compiler_params=params(57),
        name="own_half",
    )(pos, a, v)
    square, low, b_other = pl.pallas_call(
        square_kernel,
        out_shape=[shape(BLK, BS, dtype=F32), shape(BLK, BS), b_shape],
        in_specs=[SM, VM, VM, HBM, pl.BlockSpec(memory_space=pl.ANY)],
        out_specs=[VM, VM, VM],
        scratch_shapes=block_scratch,
        compiler_params=params(16),
        name="square",
    )(pos, metas, acc, a, v_other)

    near, far = col_gather(low, BLK)
    acc = pl.pallas_call(
        near_kernel,
        out_shape=acc_shape,
        in_specs=[SM] + [VM] * 9,
        out_specs=VM,
        scratch_shapes=[pltpu.VMEM((ROWS * BS, 2 * HALF), BF)],
        compiler_params=params(16),
        name="near",
    )(pos, metas, b_own, b_other, *near)
    out = pl.pallas_call(
        far_kernel,
        out_shape=shape(BLK, BS),
        in_specs=[SM] + [VM] * (5 + len(far)),
        out_specs=VM,
        scratch_shapes=[pltpu.VMEM((ROWS * BS, 4 * CG * BS), BF), pltpu.VMEM((4 * CG * BS, CG * BS), BF)],
        compiler_params=params(16),
        name="far",
    )(pos, metas, b_own, b_other, acc, square, *far)
    return out.reshape(ROWS, KD, BS, BS)


def solution(mesh):
    return jax.shard_map(
        local,
        mesh=mesh,
        in_specs=(P("row", "col", None, None), P("row", "col"), P("row", "col")),
        out_specs=P("row", "col", None, None),
        check_vma=False,
    )
```

```python
import jax
import jax.numpy as jnp
from jax import lax
from jax.experimental import pallas as pl
from jax.experimental.pallas import tpu as pltpu
from jax.sharding import PartitionSpec as P

BS = 128
KD = 3
CG = 4
ROWS = 2
NG = 16
NZ = 8
BLK = ROWS * KD * BS
PAY = BLK + 16
HALF = NG * ROWS * BS
BF = jnp.bfloat16
F32 = jnp.float32
VM = pl.BlockSpec(memory_space=pltpu.VMEM)
SM = pl.BlockSpec(memory_space=pltpu.SMEM)
HBM = pl.BlockSpec(memory_space=pltpu.HBM)

CORE_SWAP = [(r, r ^ 1) for r in range(32)]
YH_SWAP = [(r, r ^ 2) for r in range(32)]
Z_GROUPS = [[z * 4 + n for z in range(NZ)] for n in range(4)]


def yl_shift(s):
    return [(c, c // 4 * 4 + (c + s) % 4) for c in range(16)]


def x_shift(s):
    return [(c, (c + 4 * s) % 16) for c in range(16)]


def col(a, perm):
    return lax.ppermute(a, "col", perm)


def row(a, perm):
    return lax.ppermute(a, "row", perm)


def shape(*dims, dtype=BF):
    return jax.ShapeDtypeStruct(dims, dtype)


def params(mib):
    return pltpu.CompilerParams(vmem_limit_bytes=mib * 1024 * 1024)


def fence(token, *values):
    token, *values = lax.optimization_barrier((token, *values))

    def body(in_ref, out_ref):
        out_ref[...] = in_ref[...]

    token = pl.pallas_call(
        body,
        out_shape=shape(*token.shape, dtype=token.dtype),
        in_specs=[VM],
        out_specs=VM,
        compiler_params=params(1),
        cost_estimate=pl.CostEstimate(flops=4 * 10**9, bytes_accessed=0, transcendentals=0),
        name="fence",
    )(token)
    return lax.optimization_barrier((token, *values))


def cat(*arrays):
    rows = [a.shape[0] for a in arrays]

    def body(*refs):
        at = 0
        for n, ref in zip(rows, refs):
            refs[-1][at : at + n] = ref[...]
            at += n

    return pl.pallas_call(
        body,
        out_shape=shape(sum(rows), BS),
        in_specs=[VM] * len(arrays),
        out_specs=VM,
        compiler_params=params(2),
        name="cat",
    )(*arrays)


NEAR_PIECES = [
    (g * 3 + a, n, dx, dy)
    for g, dys in enumerate(((0, 3), (1, 2)))
    for a, dx in enumerate((0, 3, 1))
    for n, dy in enumerate(dys)
]
FAR_PIECES = [(0, 0, 2, 0), (1, 0, 2, 3), (2, 0, 2, 1), (3, 0, 2, 2)]
ALL_PIECES = NEAR_PIECES + [(6 + a, n, dx, dy) for a, n, dx, dy in FAR_PIECES]


def gather(own):
    token = jnp.zeros((8, BS), F32)
    own_y = row(own, YH_SWAP)
    one = cat(own, col(own, yl_shift(1)))
    token, one, own = fence(token, one, own)
    left1, right1 = [col(one, x_shift(s)) for s in (1, 3)]
    token, both, own = fence(token, cat(own, own_y), own)
    column = lax.all_gather(both, "row", axis_index_groups=Z_GROUPS, axis=0, tiled=True)
    token, two = fence(token, cat(col(own, yl_shift(3)), col(own, yl_shift(2))))
    left2, right2 = [col(two, x_shift(s)) for s in (1, 3)]
    far = [col(left1[:PAY], x_shift(1)), col(right1[PAY:], x_shift(3))]
    far += [col(left2[:PAY], x_shift(1)), col(right2[PAY:], x_shift(3))]
    return [one, left1, right1, two, left2, right2, *far], column, token


def col_gather(own, rows):
    line1, line3, line2 = [col(own, yl_shift(s)) for s in (1, 3, 2)]
    one = cat(own, line1)
    left1, right1 = col(one, x_shift(1)), col(one, x_shift(3))
    two = cat(line3, line2)
    left2, right2 = col(two, x_shift(1)), col(two, x_shift(3))
    far = [col(left1[:rows], x_shift(1)), col(right1[rows:], x_shift(3))]
    far += [col(left2[:rows], x_shift(1)), col(right2[rows:], x_shift(3))]
    return [one, left1, right1, two, left2, right2], far


def meta_rows(meta):
    wide = meta.astype(F32)
    return [
        jnp.broadcast_to(wide[s : s + 1], (16, BS)).astype(BF) for s in range(ROWS * KD)
    ]


def spread(src, base, slots, store):
    masks = [[m == jnp.full((16, BS), q, BF) for q in range(CG)] for m in slots]

    def step(n, _):
        r = pl.multiple_of(n * 16, 16)
        v = [src[pl.ds(base + t * BS + r, 16), :] for t in range(KD)]
        zero = jnp.zeros((16, BS), BF)
        for q in range(CG):
            d = zero
            for t in range(KD):
                d = jnp.where(masks[t][q], v[t], d)
            store(r, q, d)
        return 0

    lax.fori_loop(0, BS // 16, step, 0, unroll=True)


def group_of(pos, dx, dy):
    return ((pos[3] + dx) & 3) * 4 + ((pos[4] + dy) & 3)


def spread_row(pos, src, base, i, slots, group, a_ref):
    def store(r, q, d):
        half = (q >> 1) ^ pos[2]
        at = pl.multiple_of(half * HALF + group * (ROWS * BS) + (q & 1) * BS, BS)
        a_ref[pl.ds(i * BS + r, 16), pl.ds(at, BS)] = d

    spread(src, base + i * KD * BS, slots[i * KD : (i + 1) * KD], store)


def pick(acc, slots):
    out = []
    for i in range(ROWS):
        for t in range(KD):
            m = slots[i * KD + t].astype(F32)[0:1]
            d = jnp.zeros((BS, BS), F32)
            for q in range(CG):
                d = jnp.where(m == float(q), acc[i * BS : (i + 1) * BS, q * BS : (q + 1) * BS], d)
            out.append(d)
    return out


def strip_kernel(pos, token, *refs):
    cols, (a_out, meta_ref, a_ref, sems) = refs[:-4], refs[-4:]
    copies = []
    for i in range(ROWS):
        for a, n, dx, dy in ALL_PIECES:
            src, group = cols[a], group_of(pos, dx, dy)
            meta = src[n * PAY + BLK : (n + 1) * PAY]
            if i == 0:
                meta_ref[pl.ds(pl.multiple_of(group * 16, 16), 16), :] = meta
            spread_row(pos, src, n * PAY, i, meta_rows(meta), group, a_ref)
        here = pl.ds(i * BS, BS)
        copies.append(pltpu.make_async_copy(a_ref.at[here], a_out.at[here], sems.at[i]))
        copies[-1].start()
    for copy in copies:
        copy.wait()


def fetch(src, buffer, sems):
    copies = []
    for z in range(NZ):
        part = pl.ds(z * 2 * PAY, 2 * PAY)
        copies.append(pltpu.make_async_copy(src.at[part], buffer.at[part], sems.at[z]))
        copies[-1].start()
    return copies


def spread_half(pos, copies, src, b_ref):
    for z in range(NZ):
        if copies:
            copies[z].wait()
        for n in range(2):
            base = (z * 2 + n) * PAY
            slots = meta_rows(src[base + BLK : base + PAY])
            top = pl.multiple_of((z * 2 + (pos[1] ^ n)) * (ROWS * BS), ROWS * BS)
            for i in range(ROWS):

                def store(r, q, d, top=top + i * BS):
                    b_ref[pl.ds(top + r, 16), q * BS : (q + 1) * BS] = d

                spread(src, base + i * KD * BS, slots[i * KD : (i + 1) * KD], store)


def own_half_kernel(pos, a_in, v_in, acc_ref, b_ref, buffer, sems, a_ref, a_sem):
    copies = fetch(v_in, buffer, sems)
    copy = pltpu.make_async_copy(a_in.at[:, pl.ds(0, HALF)], a_ref, a_sem)
    copy.start()
    spread_half(pos, copies, buffer, b_ref)
    copy.wait()
    acc_ref[...] = jnp.dot(a_ref[...], b_ref[...], preferred_element_type=F32)


def square_kernel(pos, meta_ref, acc_ref, a_ref, v_ref, square_ref, low_ref, b_ref):
    spread_half(pos, None, v_ref, b_ref)
    acc = acc_ref[...] + jnp.dot(a_ref[:, HALF:], b_ref[...], preferred_element_type=F32)
    at = pl.multiple_of(group_of(pos, 0, 0) * 16, 16)
    for s, d in enumerate(pick(acc, meta_rows(meta_ref[pl.ds(at, 16), :]))):
        square_ref[s * BS : (s + 1) * BS] = d
        low_ref[s * BS : (s + 1) * BS] = d.astype(BF)


def near_kernel(pos, meta_ref, b_own, b_other, *refs):
    lows, acc_ref, a_ref = refs[:-2], refs[-2], refs[-1]
    for _, _, dx, dy in FAR_PIECES:
        for half in range(2):
            at = pl.multiple_of(half * HALF + group_of(pos, dx, dy) * (ROWS * BS), ROWS * BS)
            a_ref[:, pl.ds(at, ROWS * BS)] = jnp.zeros((ROWS * BS, ROWS * BS), BF)
    for a, n, dx, dy in NEAR_PIECES:
        group = group_of(pos, dx, dy)
        meta = meta_ref[pl.ds(pl.multiple_of(group * 16, 16), 16), :]
        for i in range(ROWS):
            spread_row(pos, lows[a], n * BLK, i, meta_rows(meta), group, a_ref)
    acc_ref[...] = jnp.dot(a_ref[:, :HALF], b_own[...], preferred_element_type=F32) + jnp.dot(
        a_ref[:, HALF:], b_other[...], preferred_element_type=F32
    )


def far_kernel(pos, meta_ref, b_own, b_other, acc_ref, square_ref, *refs):
    lows, (out_ref, a_ref, b_ref) = refs[:-3], refs[-3:]
    width = ROWS * BS
    for m, (a, n, dx, dy) in enumerate(FAR_PIECES):
        group = group_of(pos, dx, dy)
        at = pl.multiple_of(group * width, width)
        for half, b in enumerate((b_own, b_other)):
            b_ref[(2 * m + half) * width : (2 * m + half + 1) * width] = b[pl.ds(at, width), :]
        slots = meta_rows(meta_ref[pl.ds(pl.multiple_of(group * 16, 16), 16), :])
        for i in range(ROWS):

            def store(r, q, d, i=i, m=m):
                half = (q >> 1) ^ pos[2]
                at = pl.multiple_of((2 * m + half) * width + (q & 1) * BS, BS)
                a_ref[pl.ds(i * BS + r, 16), pl.ds(at, BS)] = d

            spread(lows[a], n * BLK + i * KD * BS, slots[i * KD : (i + 1) * KD], store)
    acc = acc_ref[...] + jnp.dot(a_ref[...], b_ref[...], preferred_element_type=F32)
    at = pl.multiple_of(group_of(pos, 0, 0) * 16, 16)
    for s, d in enumerate(pick(acc, meta_rows(meta_ref[pl.ds(at, 16), :]))):
        square = square_ref[s * BS : (s + 1) * BS]
        out_ref[s * BS : (s + 1) * BS] = (3.0 * square - 2.0 * d).astype(BF)


def local(density, block_cols, block_counts):
    slot = lax.broadcasted_iota(jnp.int32, (ROWS, KD), 1)
    where = jnp.where(slot < block_counts, block_cols % CG, -1).reshape(ROWS * KD, 1)
    meta = jnp.broadcast_to(where, (ROWS * KD, BS)).astype(BF)
    meta = jnp.pad(meta, ((0, 16 - ROWS * KD), (0, 0)))
    density = density.reshape(BLK, BS)
    own = cat(density, meta)
    r, c = lax.axis_index("row"), lax.axis_index("col")
    pos = jnp.stack([r // 4, r // 2 % 2, r % 2, c // 4, c % 4]).astype(jnp.int32)
    strips, column, token = gather(own)
    acc_shape = shape(ROWS * BS, CG * BS, dtype=F32)
    b_shape = shape(HALF, CG * BS)
    a, metas = pl.pallas_call(
        strip_kernel,
        out_shape=[shape(ROWS * BS, 2 * HALF), shape(NG * 16, BS)],
        in_specs=[SM, VM] + [VM] * len(strips),
        out_specs=[HBM, VM],
        scratch_shapes=[pltpu.VMEM((ROWS * BS, 2 * HALF), BF), pltpu.SemaphoreType.DMA((ROWS,))],
        compiler_params=params(58),
        name="strips",
    )(pos, token, *strips)
    v, a, metas = lax.optimization_barrier((column, a, metas))
    v_other = row(v, CORE_SWAP)
    acc, b_own = pl.pallas_call(
        own_half_kernel,
        out_shape=[acc_shape, b_shape],
        in_specs=[SM, HBM, HBM],
        out_specs=[VM, VM],
        scratch_shapes=[
            pltpu.VMEM((2 * NZ * PAY, BS), BF),
            pltpu.SemaphoreType.DMA((NZ,)),
            pltpu.VMEM((ROWS * BS, HALF), BF),
            pltpu.SemaphoreType.DMA(()),
        ],
        compiler_params=params(53),
        name="own_half",
    )(pos, a, v)
    square, low, b_other = pl.pallas_call(
        square_kernel,
        out_shape=[shape(BLK, BS, dtype=F32), shape(BLK, BS), b_shape],
        in_specs=[SM] + [VM] * 4,
        out_specs=[VM] * 3,
        compiler_params=params(12),
        name="square",
    )(pos, metas, acc, a, v_other)

    near, far = col_gather(low, BLK)
    acc = pl.pallas_call(
        near_kernel,
        out_shape=acc_shape,
        in_specs=[SM] + [VM] * 9,
        out_specs=VM,
        scratch_shapes=[pltpu.VMEM((ROWS * BS, 2 * HALF), BF)],
        compiler_params=params(16),
        name="near",
    )(pos, metas, b_own, b_other, *near)
    out = pl.pallas_call(
        far_kernel,
        out_shape=shape(BLK, BS),
        in_specs=[SM] + [VM] * (5 + len(far)),
        out_specs=VM,
        scratch_shapes=[pltpu.VMEM((ROWS * BS, 4 * CG * BS), BF), pltpu.VMEM((4 * CG * BS, CG * BS), BF)],
        compiler_params=params(16),
        name="far",
    )(pos, metas, b_own, b_other, acc, square, *far)
    return out.reshape(ROWS, KD, BS, BS)


def solution(mesh):
    return jax.shard_map(
        local,
        mesh=mesh,
        in_specs=(P("row", "col", None, None), P("row", "col"), P("row", "col")),
        out_specs=P("row", "col", None, None),
        check_vma=False,
    )
```

```python
import jax
import jax.numpy as jnp
from jax import lax
from jax.experimental import pallas as pl
from jax.experimental.pallas import tpu as pltpu
from jax.sharding import PartitionSpec as P

BS = 128
KD = 3
CG = 4
ROWS = 2
NG = 16
NZ = 8
BLK = ROWS * KD * BS
PAY = BLK + 16
HALF = NG * ROWS * BS
BF = jnp.bfloat16
F32 = jnp.float32
VM = pl.BlockSpec(memory_space=pltpu.VMEM)
HBM = pl.BlockSpec(memory_space=pltpu.HBM)

CORE_SWAP = [(r, r ^ 1) for r in range(32)]
YH_SWAP = [(r, r ^ 2) for r in range(32)]
Z_GROUPS = [[z * 4 + n for z in range(NZ)] for n in range(4)]


def yl_shift(s):
    return [(c, c // 4 * 4 + (c + s) % 4) for c in range(16)]


def x_step(s):
    return [
        (r * 16 + c, r * 16 + (c + 4 * s * (1 - 2 * (r % 2))) % 16) for r in range(32) for c in range(16)
    ]


AHEAD, BACK = x_step(1), x_step(-1)


def col(a, perm):
    return lax.ppermute(a, "col", perm)


def both_axes(a, perm):
    return lax.ppermute(a, ("row", "col"), perm)


def row(a, perm):
    return lax.ppermute(a, "row", perm)


def shape(*dims, dtype=BF):
    return jax.ShapeDtypeStruct(dims, dtype)


def params(mib):
    return pltpu.CompilerParams(vmem_limit_bytes=mib * 1024 * 1024)


def fence(token, *values):
    token, *values = lax.optimization_barrier((token, *values))

    def body(in_ref, out_ref):
        out_ref[...] = in_ref[...]

    token = pl.pallas_call(
        body,
        out_shape=shape(*token.shape, dtype=token.dtype),
        in_specs=[VM],
        out_specs=VM,
        compiler_params=params(1),
        cost_estimate=pl.CostEstimate(flops=4 * 10**9, bytes_accessed=0, transcendentals=0),
        name="fence",
    )(token)
    return lax.optimization_barrier((token, *values))


def cat(*arrays):
    rows = [a.shape[0] for a in arrays]

    def body(*refs):
        at = 0
        for n, ref in zip(rows, refs):
            refs[-1][at : at + n] = ref[...]
            at += n

    return pl.pallas_call(
        body,
        out_shape=shape(sum(rows), BS),
        in_specs=[VM] * len(arrays),
        out_specs=VM,
        compiler_params=params(2),
        name="cat",
    )(*arrays)


NEAR_PIECES = [
    (g * 3 + a, n, dx, dy)
    for g, dys in enumerate(((0, 3), (1, 2)))
    for a, dx in enumerate((0, -1, 1))
    for n, dy in enumerate(dys)
]
FAR_PIECES = [(0, 0, 2, 0), (0, 1, 2, 3), (1, 0, 2, 1), (1, 1, 2, 2)]
ALL_PIECES = NEAR_PIECES + [(6 + a, n, dx, dy) for a, n, dx, dy in FAR_PIECES]


def gather(own):
    token = jnp.zeros((8, BS), F32)
    own_y = row(own, YH_SWAP)
    one = cat(own, col(own, yl_shift(1)))
    token, one, own = fence(token, one, own)
    ahead1, back1 = both_axes(one, AHEAD), both_axes(one, BACK)
    token, both, own = fence(token, cat(own, own_y), own)
    column = lax.all_gather(both, "row", axis_index_groups=Z_GROUPS, axis=0, tiled=True)
    token, two = fence(token, cat(col(own, yl_shift(3)), col(own, yl_shift(2))))
    ahead2, back2 = both_axes(two, AHEAD), both_axes(two, BACK)
    ahead1, back1 = lax.optimization_barrier((ahead1, back1))
    ahead2, back2 = lax.optimization_barrier((ahead2, back2))
    far = [both_axes(ahead1, AHEAD), both_axes(ahead2, AHEAD)]
    return [one, ahead1, back1, two, ahead2, back2, *far], column, token


def col_gather(own):
    line1, line3, line2 = [col(own, yl_shift(s)) for s in (1, 3, 2)]
    one = cat(own, line1)
    ahead1, back1 = both_axes(one, AHEAD), both_axes(one, BACK)
    two = cat(line3, line2)
    ahead2, back2 = both_axes(two, AHEAD), both_axes(two, BACK)
    ahead1, back1 = lax.optimization_barrier((ahead1, back1))
    ahead2, back2 = lax.optimization_barrier((ahead2, back2))
    far = [both_axes(ahead1, AHEAD), both_axes(ahead2, AHEAD)]
    return [one, ahead1, back1, two, ahead2, back2], far


def meta_rows(meta):
    wide = meta.astype(F32)
    return [
        jnp.broadcast_to(wide[s : s + 1], (16, BS)).astype(BF) for s in range(ROWS * KD)
    ]


def spread(src, base, slots, store):
    masks = [[m == jnp.full((16, BS), q, BF) for q in range(CG)] for m in slots]

    def step(n, _):
        r = pl.multiple_of(n * 16, 16)
        v = [src[pl.ds(base + t * BS + r, 16), :] for t in range(KD)]
        zero = jnp.zeros((16, BS), BF)
        for q in range(CG):
            d = zero
            for t in range(KD):
                d = jnp.where(masks[t][q], v[t], d)
            store(r, q, d)
        return 0

    lax.fori_loop(0, BS // 16, step, 0, unroll=True)


def position():
    r, c = lax.axis_index("row"), lax.axis_index("col")
    return r >> 2, (r >> 1) & 1, r & 1, c >> 2, c & 3


def group_of(pos, dx, dy):
    return ((pos[3] + dx * (1 - 2 * pos[2])) & 3) * 4 + ((pos[4] + dy) & 3)


def spread_row(pos, src, base, i, slots, group, a_ref):
    def store(r, q, d):
        half = (q >> 1) ^ pos[2]
        at = pl.multiple_of(half * HALF + group * (ROWS * BS) + (q & 1) * BS, BS)
        a_ref[pl.ds(i * BS + r, 16), pl.ds(at, BS)] = d

    spread(src, base + i * KD * BS, slots[i * KD : (i + 1) * KD], store)


def pick(acc, slots):
    out = []
    for i in range(ROWS):
        for t in range(KD):
            m = slots[i * KD + t].astype(F32)[0:1]
            d = jnp.zeros((BS, BS), F32)
            for q in range(CG):
                d = jnp.where(m == float(q), acc[i * BS : (i + 1) * BS, q * BS : (q + 1) * BS], d)
            out.append(d)
    return out


def strip_kernel(token, *refs):
    pos = position()
    cols, (a_out, meta_ref, a_ref, sems) = refs[:-4], refs[-4:]
    copies = []
    for i in range(ROWS):
        for a, n, dx, dy in ALL_PIECES:
            src, group = cols[a], group_of(pos, dx, dy)
            meta = src[n * PAY + BLK : (n + 1) * PAY]
            if i == 0:
                meta_ref[pl.ds(pl.multiple_of(group * 16, 16), 16), :] = meta
            spread_row(pos, src, n * PAY, i, meta_rows(meta), group, a_ref)
        here = pl.ds(i * BS, BS)
        copies.append(pltpu.make_async_copy(a_ref.at[here], a_out.at[here], sems.at[i]))
        copies[-1].start()
    for copy in copies:
        copy.wait()


def fetch(src, buffer, sems):
    copies = []
    for z in range(NZ):
        part = pl.ds(z * 2 * PAY, 2 * PAY)
        copies.append(pltpu.make_async_copy(src.at[part], buffer.at[part], sems.at[z]))
        copies[-1].start()
    return copies


def spread_half(pos, copies, src, b_ref):
    for z in range(NZ):
        if copies:
            copies[z].wait()
        for n in range(2):
            base = (z * 2 + n) * PAY
            slots = meta_rows(src[base + BLK : base + PAY])
            top = pl.multiple_of((z * 2 + (pos[1] ^ n)) * (ROWS * BS), ROWS * BS)
            for i in range(ROWS):

                def store(r, q, d, top=top + i * BS):
                    b_ref[pl.ds(top + r, 16), q * BS : (q + 1) * BS] = d

                spread(src, base + i * KD * BS, slots[i * KD : (i + 1) * KD], store)


def own_half_kernel(a_in, v_in, acc_ref, b_ref, buffer, sems, a_ref, a_sem):
    pos = position()
    copies = fetch(v_in, buffer, sems)
    copy = pltpu.make_async_copy(a_in.at[:, pl.ds(0, HALF)], a_ref, a_sem)
    copy.start()
    spread_half(pos, copies, buffer, b_ref)
    copy.wait()
    acc_ref[...] = jnp.dot(a_ref[...], b_ref[...], preferred_element_type=F32)


def square_kernel(meta_ref, acc_ref, a_ref, v_ref, square_ref, low_ref, b_ref):
    pos = position()
    spread_half(pos, None, v_ref, b_ref)
    acc = acc_ref[...] + jnp.dot(a_ref[:, HALF:], b_ref[...], preferred_element_type=F32)
    at = pl.multiple_of(group_of(pos, 0, 0) * 16, 16)
    for s, d in enumerate(pick(acc, meta_rows(meta_ref[pl.ds(at, 16), :]))):
        square_ref[s * BS : (s + 1) * BS] = d
        low_ref[s * BS : (s + 1) * BS] = d.astype(BF)


def near_kernel(meta_ref, b_own, b_other, *refs):
    pos = position()
    lows, acc_ref, a_ref = refs[:-2], refs[-2], refs[-1]
    for _, _, dx, dy in FAR_PIECES:
        for half in range(2):
            at = pl.multiple_of(half * HALF + group_of(pos, dx, dy) * (ROWS * BS), ROWS * BS)
            a_ref[:, pl.ds(at, ROWS * BS)] = jnp.zeros((ROWS * BS, ROWS * BS), BF)
    for a, n, dx, dy in NEAR_PIECES:
        group = group_of(pos, dx, dy)
        meta = meta_ref[pl.ds(pl.multiple_of(group * 16, 16), 16), :]
        for i in range(ROWS):
            spread_row(pos, lows[a], n * BLK, i, meta_rows(meta), group, a_ref)
    acc_ref[...] = jnp.dot(a_ref[:, :HALF], b_own[...], preferred_element_type=F32) + jnp.dot(
        a_ref[:, HALF:], b_other[...], preferred_element_type=F32
    )


def far_kernel(meta_ref, b_own, b_other, acc_ref, square_ref, *refs):
    pos = position()
    lows, (out_ref, a_ref, b_ref) = refs[:-3], refs[-3:]
    width = ROWS * BS
    for m, (a, n, dx, dy) in enumerate(FAR_PIECES):
        group = group_of(pos, dx, dy)
        at = pl.multiple_of(group * width, width)
        for half, b in enumerate((b_own, b_other)):
            b_ref[(2 * m + half) * width : (2 * m + half + 1) * width] = b[pl.ds(at, width), :]
        slots = meta_rows(meta_ref[pl.ds(pl.multiple_of(group * 16, 16), 16), :])
        for i in range(ROWS):

            def store(r, q, d, i=i, m=m):
                half = (q >> 1) ^ pos[2]
                at = pl.multiple_of((2 * m + half) * width + (q & 1) * BS, BS)
                a_ref[pl.ds(i * BS + r, 16), pl.ds(at, BS)] = d

            spread(lows[a], n * BLK + i * KD * BS, slots[i * KD : (i + 1) * KD], store)
    acc = acc_ref[...] + jnp.dot(a_ref[...], b_ref[...], preferred_element_type=F32)
    at = pl.multiple_of(group_of(pos, 0, 0) * 16, 16)
    for s, d in enumerate(pick(acc, meta_rows(meta_ref[pl.ds(at, 16), :]))):
        square = square_ref[s * BS : (s + 1) * BS]
        out_ref[s * BS : (s + 1) * BS] = (3.0 * square - 2.0 * d).astype(BF)


def local(density, block_cols, block_counts):
    slot = lax.broadcasted_iota(jnp.int32, (ROWS, KD), 1)
    where = jnp.where(slot < block_counts, block_cols % CG, -1).reshape(ROWS * KD, 1)
    meta = jnp.broadcast_to(where, (ROWS * KD, BS)).astype(BF)
    meta = jnp.pad(meta, ((0, 16 - ROWS * KD), (0, 0)))
    density = density.reshape(BLK, BS)
    own = cat(density, meta)
    strips, column, token = gather(own)
    acc_shape = shape(ROWS * BS, CG * BS, dtype=F32)
    b_shape = shape(HALF, CG * BS)
    a, metas = pl.pallas_call(
        strip_kernel,
        out_shape=[shape(ROWS * BS, 2 * HALF), shape(NG * 16, BS)],
        in_specs=[VM] * (1 + len(strips)),
        out_specs=[HBM, VM],
        scratch_shapes=[pltpu.VMEM((ROWS * BS, 2 * HALF), BF), pltpu.SemaphoreType.DMA((ROWS,))],
        compiler_params=params(58),
        name="strips",
    )(token, *strips)
    v, a, metas = lax.optimization_barrier((column, a, metas))
    v_other = row(v, CORE_SWAP)
    acc, b_own = pl.pallas_call(
        own_half_kernel,
        out_shape=[acc_shape, b_shape],
        in_specs=[HBM, HBM],
        out_specs=[VM, VM],
        scratch_shapes=[
            pltpu.VMEM((2 * NZ * PAY, BS), BF),
            pltpu.SemaphoreType.DMA((NZ,)),
            pltpu.VMEM((ROWS * BS, HALF), BF),
            pltpu.SemaphoreType.DMA(()),
        ],
        compiler_params=params(53),
        name="own_half",
    )(a, v)
    square, low, b_other = pl.pallas_call(
        square_kernel,
        out_shape=[shape(BLK, BS, dtype=F32), shape(BLK, BS), b_shape],
        in_specs=[VM] * 4,
        out_specs=[VM] * 3,
        compiler_params=params(12),
        name="square",
    )(metas, acc, a, v_other)

    near, far = col_gather(low)
    acc = pl.pallas_call(
        near_kernel,
        out_shape=acc_shape,
        in_specs=[VM] * 9,
        out_specs=VM,
        scratch_shapes=[pltpu.VMEM((ROWS * BS, 2 * HALF), BF)],
        compiler_params=params(16),
        name="near",
    )(metas, b_own, b_other, *near)
    out = pl.pallas_call(
        far_kernel,
        out_shape=shape(BLK, BS),
        in_specs=[VM] * (5 + len(far)),
        out_specs=VM,
        scratch_shapes=[pltpu.VMEM((ROWS * BS, 4 * CG * BS), BF), pltpu.VMEM((4 * CG * BS, CG * BS), BF)],
        compiler_params=params(16),
        name="far",
    )(metas, b_own, b_other, acc, square, *far)
    return out.reshape(ROWS, KD, BS, BS)


def solution(mesh):
    return jax.shard_map(
        local,
        mesh=mesh,
        in_specs=(P("row", "col", None, None), P("row", "col"), P("row", "col")),
        out_specs=P("row", "col", None, None),
        check_vma=False,
    )
```

```python
import jax
import jax.numpy as jnp
from jax import lax
from jax.experimental import pallas as pl
from jax.experimental.pallas import tpu as pltpu
from jax.sharding import PartitionSpec as P

BS = 128
KD = 3
CG = 4
ROWS = 2
NG = 16
NZ = 8
BLK = ROWS * KD * BS
PAY = BLK + 16
HALF = NG * ROWS * BS
BF = jnp.bfloat16
F32 = jnp.float32
VM = pl.BlockSpec(memory_space=pltpu.VMEM)
HBM = pl.BlockSpec(memory_space=pltpu.HBM)

CORE_SWAP = [(r, r ^ 1) for r in range(32)]
YH_SWAP = [(r, r ^ 2) for r in range(32)]
Z_GROUPS = [[z * 4 + n for z in range(NZ)] for n in range(4)]


def yl_shift(s):
    return [(c, c // 4 * 4 + (c + s) % 4) for c in range(16)]


def x_step(s):
    return [
        (r * 16 + c, r * 16 + (c + 4 * s * (1 - 2 * (r % 2))) % 16) for r in range(32) for c in range(16)
    ]


AHEAD, BACK = x_step(1), x_step(-1)


def col(a, perm):
    return lax.ppermute(a, "col", perm)


def both_axes(a, perm):
    return lax.ppermute(a, ("row", "col"), perm)


def row(a, perm):
    return lax.ppermute(a, "row", perm)


def shape(*dims, dtype=BF):
    return jax.ShapeDtypeStruct(dims, dtype)


def params(mib):
    return pltpu.CompilerParams(vmem_limit_bytes=mib * 1024 * 1024)


def fence(token, *values):
    token, *values = lax.optimization_barrier((token, *values))

    def body(in_ref, out_ref):
        out_ref[...] = in_ref[...]

    token = pl.pallas_call(
        body,
        out_shape=shape(*token.shape, dtype=token.dtype),
        in_specs=[VM],
        out_specs=VM,
        compiler_params=params(1),
        cost_estimate=pl.CostEstimate(flops=4 * 10**9, bytes_accessed=0, transcendentals=0),
        name="fence",
    )(token)
    return lax.optimization_barrier((token, *values))


def cat(*arrays):
    rows = [a.shape[0] for a in arrays]

    def body(*refs):
        at = 0
        for n, ref in zip(rows, refs):
            refs[-1][at : at + n] = ref[...]
            at += n

    return pl.pallas_call(
        body,
        out_shape=shape(sum(rows), BS),
        in_specs=[VM] * len(arrays),
        out_specs=VM,
        compiler_params=params(2),
        name="cat",
    )(*arrays)


NEAR_PIECES = [
    (g * 3 + a, n, dx, dy)
    for g, dys in enumerate(((0, 3), (1, 2)))
    for a, dx in enumerate((0, -1, 1))
    for n, dy in enumerate(dys)
]
FAR_PIECES = [(0, 0, 2, 0), (0, 1, 2, 3), (1, 0, 2, 1), (1, 1, 2, 2)]
ALL_PIECES = NEAR_PIECES + [(6 + a, n, dx, dy) for a, n, dx, dy in FAR_PIECES]


def gather(own):
    token = jnp.zeros((8, BS), F32)
    own_y = row(own, YH_SWAP)
    one = cat(own, col(own, yl_shift(1)))
    token, one, own = fence(token, one, own)
    ahead1, back1 = both_axes(one, AHEAD), both_axes(one, BACK)
    token, both, own = fence(token, cat(own, own_y), own)
    column = lax.all_gather(both, "row", axis_index_groups=Z_GROUPS, axis=0, tiled=True)
    token, two = fence(token, cat(col(own, yl_shift(3)), col(own, yl_shift(2))))
    ahead2, back2 = both_axes(two, AHEAD), both_axes(two, BACK)
    ahead1, back1 = lax.optimization_barrier((ahead1, back1))
    ahead2, back2 = lax.optimization_barrier((ahead2, back2))
    far = [both_axes(ahead1, AHEAD), both_axes(ahead2, AHEAD)]
    return [one, ahead1, back1, two, ahead2, back2, *far], column, token


def col_gather(own):
    line1, line3, line2 = [col(own, yl_shift(s)) for s in (1, 3, 2)]
    one = cat(own, line1)
    ahead1, back1 = both_axes(one, AHEAD), both_axes(one, BACK)
    two = cat(line3, line2)
    ahead2, back2 = both_axes(two, AHEAD), both_axes(two, BACK)
    ahead1, back1 = lax.optimization_barrier((ahead1, back1))
    far = [both_axes(ahead1, AHEAD), both_axes(ahead2, AHEAD)]
    return [one, ahead1, back1, two, ahead2, back2], far


def meta_rows(meta):
    wide = meta.astype(F32)
    return [
        jnp.broadcast_to(wide[s : s + 1], (16, BS)).astype(BF) for s in range(ROWS * KD)
    ]


def spread(src, base, slots, store):
    masks = [[m == jnp.full((16, BS), q, BF) for q in range(CG)] for m in slots]

    def step(n, _):
        r = pl.multiple_of(n * 16, 16)
        v = [src[pl.ds(base + t * BS + r, 16), :] for t in range(KD)]
        zero = jnp.zeros((16, BS), BF)
        for q in range(CG):
            d = zero
            for t in range(KD):
                d = jnp.where(masks[t][q], v[t], d)
            store(r, q, d)
        return 0

    lax.fori_loop(0, BS // 16, step, 0, unroll=True)


def position():
    r, c = lax.axis_index("row"), lax.axis_index("col")
    return r >> 2, (r >> 1) & 1, r & 1, c >> 2, c & 3


def group_of(pos, dx, dy):
    return ((pos[3] + dx * (1 - 2 * pos[2])) & 3) * 4 + ((pos[4] + dy) & 3)


def spread_row(pos, src, base, i, slots, group, a_ref):
    def store(r, q, d):
        half = (q >> 1) ^ pos[2]
        at = pl.multiple_of(half * HALF + group * (ROWS * BS) + (q & 1) * BS, BS)
        a_ref[pl.ds(i * BS + r, 16), pl.ds(at, BS)] = d

    spread(src, base + i * KD * BS, slots[i * KD : (i + 1) * KD], store)


def pick(acc, slots):
    out = []
    for i in range(ROWS):
        for t in range(KD):
            m = slots[i * KD + t].astype(F32)[0:1]
            d = jnp.zeros((BS, BS), F32)
            for q in range(CG):
                d = jnp.where(m == float(q), acc[i * BS : (i + 1) * BS, q * BS : (q + 1) * BS], d)
            out.append(d)
    return out


def strip_kernel(token, *refs):
    pos = position()
    cols, (a_out, meta_ref, a_ref, sems) = refs[:-4], refs[-4:]
    copies = []
    for i in range(ROWS):
        for a, n, dx, dy in ALL_PIECES:
            src, group = cols[a], group_of(pos, dx, dy)
            meta = src[n * PAY + BLK : (n + 1) * PAY]
            if i == 0:
                meta_ref[pl.ds(pl.multiple_of(group * 16, 16), 16), :] = meta
            spread_row(pos, src, n * PAY, i, meta_rows(meta), group, a_ref)
        here = pl.ds(i * BS, BS)
        copies.append(pltpu.make_async_copy(a_ref.at[here], a_out.at[here], sems.at[i]))
        copies[-1].start()
    for copy in copies:
        copy.wait()


def fetch(src, buffer, sems):
    copies = []
    for z in range(NZ):
        part = pl.ds(z * 2 * PAY, 2 * PAY)
        copies.append(pltpu.make_async_copy(src.at[part], buffer.at[part], sems.at[z]))
        copies[-1].start()
    return copies


def spread_half(pos, copies, src, b_ref):
    for z in range(NZ):
        if copies:
            copies[z].wait()
        for n in range(2):
            base = (z * 2 + n) * PAY
            slots = meta_rows(src[base + BLK : base + PAY])
            top = pl.multiple_of((z * 2 + (pos[1] ^ n)) * (ROWS * BS), ROWS * BS)
            for i in range(ROWS):

                def store(r, q, d, top=top + i * BS):
                    b_ref[pl.ds(top + r, 16), q * BS : (q + 1) * BS] = d

                spread(src, base + i * KD * BS, slots[i * KD : (i + 1) * KD], store)


def own_half_kernel(a_in, v_in, acc_ref, b_ref, buffer, sems, a_ref, a_sem):
    pos = position()
    copies = fetch(v_in, buffer, sems)
    copy = pltpu.make_async_copy(a_in.at[:, pl.ds(0, HALF)], a_ref, a_sem)
    copy.start()
    spread_half(pos, copies, buffer, b_ref)
    copy.wait()
    acc_ref[...] = jnp.dot(a_ref[...], b_ref[...], preferred_element_type=F32)


def square_kernel(meta_ref, acc_ref, a_ref, v_ref, square_ref, low_ref, b_ref):
    pos = position()
    spread_half(pos, None, v_ref, b_ref)
    acc = acc_ref[...] + jnp.dot(a_ref[:, HALF:], b_ref[...], preferred_element_type=F32)
    at = pl.multiple_of(group_of(pos, 0, 0) * 16, 16)
    for s, d in enumerate(pick(acc, meta_rows(meta_ref[pl.ds(at, 16), :]))):
        square_ref[s * BS : (s + 1) * BS] = d
        low_ref[s * BS : (s + 1) * BS] = d.astype(BF)


def near_kernel(meta_ref, b_own, b_other, *refs):
    pos = position()
    lows, acc_ref, a_ref = refs[:-2], refs[-2], refs[-1]
    for _, _, dx, dy in FAR_PIECES:
        for half in range(2):
            at = pl.multiple_of(half * HALF + group_of(pos, dx, dy) * (ROWS * BS), ROWS * BS)
            a_ref[:, pl.ds(at, ROWS * BS)] = jnp.zeros((ROWS * BS, ROWS * BS), BF)
    for a, n, dx, dy in NEAR_PIECES:
        group = group_of(pos, dx, dy)
        meta = meta_ref[pl.ds(pl.multiple_of(group * 16, 16), 16), :]
        for i in range(ROWS):
            spread_row(pos, lows[a], n * BLK, i, meta_rows(meta), group, a_ref)
    acc_ref[...] = jnp.dot(a_ref[:, :HALF], b_own[...], preferred_element_type=F32) + jnp.dot(
        a_ref[:, HALF:], b_other[...], preferred_element_type=F32
    )


def far_kernel(meta_ref, b_own, b_other, acc_ref, square_ref, *refs):
    pos = position()
    lows, (out_ref, a_ref, b_ref) = refs[:-3], refs[-3:]
    width = ROWS * BS
    for m, (a, n, dx, dy) in enumerate(FAR_PIECES):
        group = group_of(pos, dx, dy)
        at = pl.multiple_of(group * width, width)
        for half, b in enumerate((b_own, b_other)):
            b_ref[(2 * m + half) * width : (2 * m + half + 1) * width] = b[pl.ds(at, width), :]
        slots = meta_rows(meta_ref[pl.ds(pl.multiple_of(group * 16, 16), 16), :])
        for i in range(ROWS):

            def store(r, q, d, i=i, m=m):
                half = (q >> 1) ^ pos[2]
                at = pl.multiple_of((2 * m + half) * width + (q & 1) * BS, BS)
                a_ref[pl.ds(i * BS + r, 16), pl.ds(at, BS)] = d

            spread(lows[a], n * BLK + i * KD * BS, slots[i * KD : (i + 1) * KD], store)
    acc = acc_ref[...] + jnp.dot(a_ref[...], b_ref[...], preferred_element_type=F32)
    at = pl.multiple_of(group_of(pos, 0, 0) * 16, 16)
    for s, d in enumerate(pick(acc, meta_rows(meta_ref[pl.ds(at, 16), :]))):
        square = square_ref[s * BS : (s + 1) * BS]
        out_ref[s * BS : (s + 1) * BS] = (3.0 * square - 2.0 * d).astype(BF)


def local(density, block_cols, block_counts):
    slot = lax.broadcasted_iota(jnp.int32, (ROWS, KD), 1)
    where = jnp.where(slot < block_counts, block_cols % CG, -1).reshape(ROWS * KD, 1)
    meta = jnp.broadcast_to(where, (ROWS * KD, BS)).astype(BF)
    meta = jnp.pad(meta, ((0, 16 - ROWS * KD), (0, 0)))
    density = density.reshape(BLK, BS)
    own = cat(density, meta)
    strips, column, token = gather(own)
    acc_shape = shape(ROWS * BS, CG * BS, dtype=F32)
    b_shape = shape(HALF, CG * BS)
    a, metas = pl.pallas_call(
        strip_kernel,
        out_shape=[shape(ROWS * BS, 2 * HALF), shape(NG * 16, BS)],
        in_specs=[VM] * (1 + len(strips)),
        out_specs=[HBM, VM],
        scratch_shapes=[pltpu.VMEM((ROWS * BS, 2 * HALF), BF), pltpu.SemaphoreType.DMA((ROWS,))],
        compiler_params=params(58),
        name="strips",
    )(token, *strips)
    v, a, metas = lax.optimization_barrier((column, a, metas))
    v_other = row(v, CORE_SWAP)
    acc, b_own = pl.pallas_call(
        own_half_kernel,
        out_shape=[acc_shape, b_shape],
        in_specs=[HBM, HBM],
        out_specs=[VM, VM],
        scratch_shapes=[
            pltpu.VMEM((2 * NZ * PAY, BS), BF),
            pltpu.SemaphoreType.DMA((NZ,)),
            pltpu.VMEM((ROWS * BS, HALF), BF),
            pltpu.SemaphoreType.DMA(()),
        ],
        compiler_params=params(53),
        name="own_half",
    )(a, v)
    square, low, b_other = pl.pallas_call(
        square_kernel,
        out_shape=[shape(BLK, BS, dtype=F32), shape(BLK, BS), b_shape],
        in_specs=[VM] * 4,
        out_specs=[VM] * 3,
        compiler_params=params(12),
        name="square",
    )(metas, acc, a, v_other)

    near, far = col_gather(low)
    acc = pl.pallas_call(
        near_kernel,
        out_shape=acc_shape,
        in_specs=[VM] * 9,
        out_specs=VM,
        scratch_shapes=[pltpu.VMEM((ROWS * BS, 2 * HALF), BF)],
        compiler_params=params(16),
        name="near",
    )(metas, b_own, b_other, *near)
    out = pl.pallas_call(
        far_kernel,
        out_shape=shape(BLK, BS),
        in_specs=[VM] * (5 + len(far)),
        out_specs=VM,
        scratch_shapes=[pltpu.VMEM((ROWS * BS, 4 * CG * BS), BF), pltpu.VMEM((4 * CG * BS, CG * BS), BF)],
        compiler_params=params(16),
        name="far",
    )(metas, b_own, b_other, acc, square, *far)
    return out.reshape(ROWS, KD, BS, BS)


def solution(mesh):
    return jax.shard_map(
        local,
        mesh=mesh,
        in_specs=(P("row", "col", None, None), P("row", "col"), P("row", "col")),
        out_specs=P("row", "col", None, None),
        check_vma=False,
    )
```
